32 devices in a mesh: grp: 2 (over x), inst: 8 (over z, y), tp: 2 (over core).
Axes of the slice: x: 2, y: 2, z: 4, core: 2. Of those that a mesh axis runs over, the one named last changes fastest.
Arguments:
- key_pool: bfloat16 [640, 8, 128, 128], P(('grp', 'inst'), 'tp'), parts along dimension 0, may hold values from -5 to 5
- value_pool: bfloat16 [640, 8, 128, 128], P(('grp', 'inst'), 'tp'), parts along dimension 0, may hold values from -5 to 5
- block_table: int32 [256, 4], P(('grp', 'inst')), parts along dimension 0, may hold values from 0 to 39, as said below
- lengths: int32 [16, 16], P('grp'), parts along dimension 0, may hold values from 1 to 512, as said below
- pairs: int32 [8, 3], P('grp'), parts along dimension 0, may hold values from 0 to 15, as said below
- queries: bfloat16 [256, 2, 64, 128], P(('grp', 'inst'), None, 'tp'), parts along dimension 0, may hold values from -100 to 100
- new_keys: bfloat16 [256, 2, 8, 128], P(('grp', 'inst'), None, 'tp'), parts along dimension 0, may hold values from -4 to 4
- new_values: bfloat16 [256, 2, 8, 128], P(('grp', 'inst'), None, 'tp'), parts along dimension 0, may hold values from -5 to 5
- guest_queries: bfloat16 [16, 2, 64, 128], P(('grp', 'inst'), None, 'tp'), parts along dimension 0, may hold values from -5 to 5
- guest_new_keys: bfloat16 [16, 2, 8, 128], P(('grp', 'inst'), None, 'tp'), parts along dimension 0, may hold values from -5 to 5
- guest_new_values: bfloat16 [16, 2, 8, 128], P(('grp', 'inst'), None, 'tp'), parts along dimension 0, may hold values from -5 to 5
Outputs:
- attended: bfloat16 [256, 2, 64, 128], P(('grp', 'inst'), None, 'tp'), parts along dimension 0
- guest_keys: bfloat16 [64, 8, 128, 128], P(('grp', 'inst'), 'tp'), parts along dimension 0
- guest_values: bfloat16 [64, 8, 128, 128], P(('grp', 'inst'), 'tp'), parts along dimension 0
The draws below stay inside these ranges and needn't reach their ends.
There are 2 independent parts, one for each index of `grp`. The reference program is written for one: setup_inputs(seed, part) draws one part's arguments, and reference() takes and returns one part's arrays. A program takes and returns all parts, laid end to end along the dimension named above; each array names one. Nothing has to cross between parts.
Inputs may be any that keep to these rules, and one draw needn't show every extreme that they name: `block_table`: entries index the instance's own 40 pool blocks; the blocks that hold positions below a request's length are distinct within an instance. The lengths of one instance together take at most 40 blocks of 128 positions; the largest is reached in every draw. `pairs`: row p concerns instances p and p + 4: one is the source, the other the destination. The moved request's length is at most 510, and equals it in some row of every draw.
All inputs are finite; a program needn't handle non-finite values.
Results may differ from the reference program's by a relative error of at most 0.0049.
Values may be sent and summed in bfloat16 or wider, within the bound.
No kernel may reach another device: no remote copies, remote signals or barrier semaphores. Data moves between devices by JAX's collectives and lax.ppermute only.
A program may use at most 128 MiB of HBM per device.

```python
import math
import jax
import jax.numpy as jnp
from jax import lax

QH = 64
KVH = 8
HD = 128
R = 16
BLK = 128
MAXB = 4
STEPS = 2
POOL = 40
N_INST = 8


def pair_plan(key):
    half_cycle = N_INST // 2
    heavy_bit = jax.random.randint(jax.random.fold_in(key, 11), (half_cycle,), 0, 2)
    first_half = jnp.arange(half_cycle, dtype=jnp.int32)
    sources = first_half + heavy_bit * half_cycle
    targets = first_half + (1 - heavy_bit) * half_cycle
    widest = jax.random.randint(jax.random.fold_in(key, 15), (), 0, half_cycle)
    moved_rows = jax.random.randint(jax.random.fold_in(key, 12), (half_cycle,), 0, R)
    moved_rows = jnp.where(first_half == widest, R - 1, moved_rows)
    long_rows = (moved_rows + jax.random.randint(jax.random.fold_in(key, 13), (half_cycle,), 1, R)) % R
    capacity = MAXB * BLK
    floor_len = (MAXB - 1) * BLK + 1
    moved_len = jax.random.randint(jax.random.fold_in(key, 14), (half_cycle,), floor_len, capacity - STEPS + 1)
    moved_len = jnp.where(first_half == widest, capacity - STEPS, moved_len)
    long_len = jax.random.randint(jax.random.fold_in(key, 16), (half_cycle,), floor_len, capacity + 1)
    longest = jax.random.randint(jax.random.fold_in(key, 17), (), 0, half_cycle)
    long_len = jnp.where(first_half == longest, capacity, long_len)
    instance_ids = jnp.arange(N_INST, dtype=jnp.int32)
    pair_of = instance_ids % half_cycle
    is_heavy = sources[pair_of] == instance_ids
    row_ids = jnp.arange(R, dtype=jnp.int32)
    block_span = jax.random.randint(jax.random.fold_in(key, 18), (N_INST, R), 1, 3)
    within = jax.random.randint(jax.random.fold_in(key, 19), (N_INST, R), 1, BLK + 1)
    light_len = jax.random.randint(jax.random.fold_in(key, 20), (N_INST, R), 1, BLK // 2 + 1)
    drawn_len = jnp.where(is_heavy[:, None], (block_span - 1) * BLK + within, light_len)
    is_moved = is_heavy[:, None] & (row_ids[None, :] == moved_rows[pair_of][:, None])
    is_long = is_heavy[:, None] & (row_ids[None, :] == long_rows[pair_of][:, None])
    lengths = jnp.where(is_moved, moved_len[pair_of][:, None], jnp.where(is_long, long_len[pair_of][:, None], drawn_len))
    return (sources, moved_rows, targets, lengths.astype(jnp.int32))


def token_plan(key):
    row_count = N_INST * R
    base_keys = jax.random.truncated_normal(jax.random.fold_in(key, 41), -4.0, 4.0, (row_count, STEPS, KVH, HD), jnp.float32)
    return base_keys


def permute_pool(subkey):
    return jax.random.permutation(subkey, POOL)


def draw_lengths(key, part):
    plan = pair_plan(key)
    return plan[3]


def draw_pairs(key, part):
    sources, moved_rows, targets, lengths = pair_plan(key)
    return jnp.stack((sources, moved_rows, targets), axis=1).astype(jnp.int32)


def draw_block_table(key, part):
    lengths = pair_plan(key)[3]
    key = jax.random.fold_in(key, 31)
    spans = (lengths + BLK - 1) // BLK
    offsets = jnp.cumsum(spans, axis=1) - spans
    orders = jax.vmap(permute_pool)(jax.random.split(key, N_INST))
    picks = offsets[:, :, None] + jnp.arange(MAXB, dtype=jnp.int32)[None, None, :]
    picks = jnp.minimum(picks, POOL - 1).reshape(N_INST, R * MAXB)
    table = jnp.take_along_axis(orders, picks, axis=1)
    return table.reshape(N_INST * R, MAXB).astype(jnp.int32)


def draw_new_keys(key, part):
    base_keys = token_plan(key)
    return base_keys.astype(jnp.bfloat16)


def draw_queries(key, part):
    key = jax.random.fold_in(key, 61)
    shape = (N_INST * R, STEPS, QH, HD)
    values = jax.random.truncated_normal(key, -4.0, 4.0, shape, jnp.float32)
    return values.astype(jnp.bfloat16)


def shard_levels(stream_key, dims, shards, least, top_value):
    def one(dim, parts):
        draws = jax.random.uniform(jax.random.fold_in(jax.random.fold_in(stream_key, 6), dim), (parts,), jnp.float32, least / len(shards), top_value / len(shards))
        return jnp.repeat(jnp.exp(draws), dims[dim] // parts).reshape((-1,) + (1,) * (len(dims) - dim - 1))

    loudness = one(*shards[0])
    for cut in shards[1:]:
        loudness = loudness * one(*cut)
    return loudness


def centred(stream_key, dims, deviation, reach, cuts=(), kind=jnp.bfloat16):
    level = shard_levels(stream_key, dims, cuts, -0.22, 0.18) if cuts else 1.0
    values = jax.random.normal(stream_key, dims, jnp.float32) * deviation * level
    return jnp.minimum(jnp.maximum(values, -reach), reach).astype(kind)


def setup_inputs(seed: int = 0, part: int = 0) -> dict:
    splits = jax.random.split(jax.random.key(seed), 12)
    part_keys = jax.random.split(jax.random.fold_in(splits[11], part), 12)
    return {
        "key_pool": centred(part_keys[0], (N_INST * POOL, KVH, BLK, HD), 1.0, 5.0, ((0, 8), (1, 2))),
        "value_pool": centred(part_keys[1], (N_INST * POOL, KVH, BLK, HD), 1.0, 5.0, ((0, 8), (1, 2))),
        "block_table": draw_block_table(jax.random.fold_in(jax.random.fold_in(splits[11], part), 71), part),
        "lengths": draw_lengths(jax.random.fold_in(jax.random.fold_in(splits[11], part), 71), part),
        "pairs": draw_pairs(jax.random.fold_in(jax.random.fold_in(splits[11], part), 71), part),
        "queries": draw_queries(jax.random.fold_in(jax.random.fold_in(splits[11], part), 71), part),
        "new_keys": draw_new_keys(jax.random.fold_in(jax.random.fold_in(splits[11], part), 71), part),
        "new_values": centred(part_keys[7], (N_INST * R, STEPS, KVH, HD), 1.0, 5.0, ((0, 8), (2, 2))),
        "guest_queries": centred(part_keys[8], (N_INST, STEPS, QH, HD), 1.0, 5.0, ((0, 8), (2, 2))),
        "guest_new_keys": centred(part_keys[9], (N_INST, STEPS, KVH, HD), 1.0, 5.0, ((0, 8), (2, 2))),
        "guest_new_values": centred(part_keys[10], (N_INST, STEPS, KVH, HD), 1.0, 5.0, ((0, 8), (2, 2))),
    }


masked_score = -1e+30

def attend_one(key_blocks, value_blocks, length, query_tokens, recent_keys, recent_values):
    step_count, head_count, head_width = query_tokens.shape
    kv_count = key_blocks.shape[1]
    group_size = head_count // kv_count
    block_count = key_blocks.shape[0]
    block_len = key_blocks.shape[2]
    score_scale = 1.0 / math.sqrt(head_width)
    grouped = query_tokens.astype(jnp.float32).reshape(step_count, kv_count, group_size, head_width)
    context = jnp.einsum('sgqd,bgtd->sgqbt', grouped, key_blocks.astype(jnp.float32)) * score_scale
    position = jnp.arange(block_count, dtype=jnp.int32)[:, None] * block_len + jnp.arange(block_len, dtype=jnp.int32)[None, :]
    context = jnp.where(position < length, context, masked_score)
    recent = jnp.einsum('sgqd,tgd->sgqt', grouped, recent_keys.astype(jnp.float32)) * score_scale
    causal = jnp.arange(step_count)[None, :] <= jnp.arange(step_count)[:, None]
    recent = jnp.where(causal[:, None, None, :], recent, masked_score)
    highest = jnp.maximum(lax.optimization_barrier(jnp.max(context, axis=(3, 4))), lax.optimization_barrier(jnp.max(recent, axis=3)))
    context_exp = jnp.exp(context - highest[..., None, None])
    recent_exp = jnp.exp(recent - highest[..., None])
    denominator = lax.optimization_barrier(jnp.sum(context_exp, axis=(3, 4))) + lax.optimization_barrier(jnp.sum(recent_exp, axis=3))
    context_weight = (context_exp / denominator[..., None, None]).astype(jnp.bfloat16)
    recent_weight = (recent_exp / denominator[..., None]).astype(jnp.bfloat16)
    result_sum = jnp.einsum('sgqbt,bgtd->sgqd', context_weight.astype(jnp.float32), value_blocks.astype(jnp.float32))
    result_sum = result_sum + jnp.einsum('sgqt,tgd->sgqd', recent_weight.astype(jnp.float32), recent_values.astype(jnp.float32))
    return result_sum.astype(jnp.bfloat16).reshape(step_count, head_count, head_width)

def guest_block(blocks, length, recent_rows):
    block_count, kv_count, block_len, head_width = blocks.shape
    position = jnp.arange(block_count, dtype=jnp.int32)[:, None] * block_len + jnp.arange(block_len, dtype=jnp.int32)[None, :]
    position = position[:, None, :, None]
    filled = jnp.where(position < length, blocks, jnp.zeros_like(blocks))
    for step_index in range(recent_rows.shape[0]):
        filled = jnp.where(position == length + step_index, recent_rows[step_index][None, :, None, :], filled)
    return filled

def reference(key_pool, value_pool, block_table, lengths, pairs, queries, new_keys, new_values, guest_queries, guest_new_keys, guest_new_values):
    instances = lengths.shape[0]
    key_pools = key_pool.reshape(instances, POOL, KVH, BLK, HD)
    value_pools = value_pool.reshape(instances, POOL, KVH, BLK, HD)
    tables = block_table.reshape(instances, R, MAXB)
    query_rows = queries.reshape(instances, R, STEPS, QH, HD)
    recent_key_rows = new_keys.reshape(instances, R, STEPS, KVH, HD)
    recent_value_rows = new_values.reshape(instances, R, STEPS, KVH, HD)

    def serve_instance(inputs):
        pool_keys, pool_values, block_rows, length_row, query_block, key_block, value_block = inputs
        return jax.vmap(attend_one)(pool_keys[block_rows], pool_values[block_rows], length_row, query_block, key_block, value_block)
    attended = lax.map(serve_instance, (key_pools, value_pools, tables, lengths, query_rows, recent_key_rows, recent_value_rows))

    def migrate(inputs):
        source, request, target = inputs
        table_row = tables[source, request]
        moved_keys = key_pools[source, table_row]
        moved_values = value_pools[source, table_row]
        length = lengths[source, request]
        result = attend_one(moved_keys, moved_values, length, guest_queries[target], guest_new_keys[target], guest_new_values[target])
        return (result, guest_block(moved_keys, length, guest_new_keys[target]), guest_block(moved_values, length, guest_new_values[target]))
    sources = pairs[:, 0]
    requests = pairs[:, 1]
    targets = pairs[:, 2]
    moved_out, moved_keys, moved_values = lax.map(migrate, (sources, requests, targets))
    attended = attended.at[sources, requests].set(moved_out)
    guest_keys = jnp.zeros((instances, MAXB, KVH, BLK, HD), key_pool.dtype).at[targets].set(moved_keys)
    guest_values = jnp.zeros((instances, MAXB, KVH, BLK, HD), value_pool.dtype).at[targets].set(moved_values)
    return (attended.reshape(instances * R, STEPS, QH, HD), guest_keys.reshape(instances * MAXB, KVH, BLK, HD), guest_values.reshape(instances * MAXB, KVH, BLK, HD))
```

```python
import math

import jax
import jax.numpy as jnp
from jax import lax
from jax.experimental import pallas as pl
from jax.experimental.pallas import tpu as pltpu
from jax.sharding import PartitionSpec as P

masked_score = -1e30


def passed_along(value, axis, steps):
    count = lax.axis_size(axis)
    pairs = [(source, (source + steps) % count) for source in range(count)]
    return lax.ppermute(value, axis, pairs)


def attend_batch(key_blocks, value_blocks, length, query_tokens, recent_keys, recent_values):
    row_count, step_count, head_count, head_width = query_tokens.shape
    kv_count = key_blocks.shape[2]
    group_size = head_count // kv_count
    block_count = key_blocks.shape[1]
    block_len = key_blocks.shape[3]
    score_scale = 1.0 / math.sqrt(head_width)
    grouped = query_tokens.reshape(row_count, step_count, kv_count, group_size, head_width)
    context = (
        jnp.einsum("rsgqd,rbgtd->rsgqbt", grouped, key_blocks, preferred_element_type=jnp.float32)
        * score_scale
    )
    position = (
        jnp.arange(block_count, dtype=jnp.int32)[:, None] * block_len
        + jnp.arange(block_len, dtype=jnp.int32)[None, :]
    )
    valid = position[None] < length[:, None, None]
    context = jnp.where(valid[:, None, None, None], context, masked_score)
    recent = (
        jnp.einsum("rsgqd,rtgd->rsgqt", grouped, recent_keys, preferred_element_type=jnp.float32)
        * score_scale
    )
    causal = jnp.arange(step_count)[None, :] <= jnp.arange(step_count)[:, None]
    recent = jnp.where(causal[None, :, None, None, :], recent, masked_score)
    highest = jnp.maximum(jnp.max(context, axis=(4, 5)), jnp.max(recent, axis=4))
    context_exp = jnp.exp(context - highest[..., None, None])
    recent_exp = jnp.exp(recent - highest[..., None])
    denominator = jnp.sum(context_exp, axis=(4, 5)) + jnp.sum(recent_exp, axis=4)
    context_weight = (context_exp / denominator[..., None, None]).astype(jnp.bfloat16)
    recent_weight = (recent_exp / denominator[..., None]).astype(jnp.bfloat16)
    result_sum = jnp.einsum(
        "rsgqbt,rbgtd->rsgqd", context_weight, value_blocks, preferred_element_type=jnp.float32
    )
    result_sum = result_sum + jnp.einsum(
        "rsgqt,rtgd->rsgqd", recent_weight, recent_values, preferred_element_type=jnp.float32
    )
    return result_sum.astype(jnp.bfloat16).reshape(row_count, step_count, head_count, head_width)


def guest_block(blocks, length, recent_rows):
    block_count, kv_count, block_len, head_width = blocks.shape
    position = (
        jnp.arange(block_count, dtype=jnp.int32)[:, None] * block_len
        + jnp.arange(block_len, dtype=jnp.int32)[None, :]
    )
    position = position[:, None, :, None]
    filled = jnp.where(position < length, blocks, jnp.zeros_like(blocks))
    for step_index in range(recent_rows.shape[0]):
        filled = jnp.where(
            position == length + step_index, recent_rows[step_index][None, :, None, :], filled
        )
    return filled


def pick_kernel(blocks, half_cycle, pairs_ref, table_ref, key_ref, value_ref, keys_out, values_out, sems):
    row = lax.rem(lax.axis_index("inst"), half_cycle)
    request = pairs_ref[row, 1]
    copies = []
    for block in range(blocks):
        place = table_ref[block, request]
        copies.append(pltpu.make_async_copy(key_ref.at[place], keys_out.at[block], sems.at[block]))
        copies.append(
            pltpu.make_async_copy(value_ref.at[place], values_out.at[block], sems.at[blocks + block])
        )
    for copy in copies:
        copy.start()
    for copy in copies:
        copy.wait()


def pick_moved(key_pool, value_pool, block_table, pairs, half_cycle):
    blocks = block_table.shape[1]
    shape = jax.ShapeDtypeStruct((blocks,) + key_pool.shape[1:], key_pool.dtype)
    smem = pl.BlockSpec(memory_space=pltpu.SMEM)
    anywhere = pl.BlockSpec(memory_space=pl.ANY)
    pool = pl.BlockSpec(memory_space=pltpu.HBM)
    return pl.pallas_call(
        lambda *refs: pick_kernel(blocks, half_cycle, *refs),
        out_shape=(shape, shape),
        in_specs=[smem, smem, pool, pool],
        out_specs=(anywhere, anywhere),
        scratch_shapes=[pltpu.SemaphoreType.DMA((2 * blocks,))],
        name="pick_moved",
    )(pairs, block_table.T, key_pool, value_pool)


def shards(
    key_pool,
    value_pool,
    block_table,
    lengths,
    pairs,
    queries,
    new_keys,
    new_values,
    guest_queries,
    guest_new_keys,
    guest_new_values,
):
    half_cycle = lax.axis_size("inst") // 2
    own_index = lax.axis_index("inst")
    send_keys, send_values = pick_moved(key_pool, value_pool, block_table, pairs, half_cycle)
    got_keys = passed_along(send_keys, "inst", half_cycle)
    got_values = passed_along(send_values, "inst", half_cycle)
    guest_tokens = jnp.concatenate([guest_queries, guest_new_keys, guest_new_values], axis=2)
    moved_tokens = passed_along(guest_tokens, "inst", half_cycle)
    head_count = queries.shape[2]
    kv_count = new_keys.shape[2]

    pair_row = lax.dynamic_index_in_dim(pairs, own_index % half_cycle, 0, keepdims=False)
    source = pair_row[0]
    request = pair_row[1]
    target = pair_row[2]
    own_lengths = lax.dynamic_index_in_dim(lengths, own_index, 0, keepdims=False)
    source_lengths = lax.dynamic_index_in_dim(lengths, source, 0, keepdims=False)
    moved_length = lax.dynamic_index_in_dim(source_lengths, request, 0, keepdims=False)
    row_ids = jnp.arange(own_lengths.shape[0], dtype=jnp.int32)
    replace = ((source == own_index) & (row_ids == request))[:, None, None, None]
    attended = attend_batch(
        key_pool[block_table],
        value_pool[block_table],
        own_lengths,
        jnp.where(replace, moved_tokens[:, :, :head_count], queries),
        jnp.where(replace, moved_tokens[:, :, head_count : head_count + kv_count], new_keys),
        jnp.where(replace, moved_tokens[:, :, head_count + kv_count :], new_values),
    )
    receiving = target == own_index
    guest_length = jnp.where(receiving, moved_length, -guest_new_keys.shape[1])
    guest_keys = guest_block(got_keys, guest_length, guest_new_keys[0])
    guest_keys, got_values = lax.optimization_barrier((guest_keys, got_values))
    guest_values = guest_block(got_values, guest_length, guest_new_values[0])
    return (attended, guest_keys, guest_values)


def solution(mesh):
    return jax.shard_map(
        shards,
        mesh=mesh,
        in_specs=(
            P(("grp", "inst"), "tp", None, None),
            P(("grp", "inst"), "tp", None, None),
            P(("grp", "inst"), None),
            P("grp", None),
            P("grp", None),
            P(("grp", "inst"), None, "tp", None),
            P(("grp", "inst"), None, "tp", None),
            P(("grp", "inst"), None, "tp", None),
            P(("grp", "inst"), None, "tp", None),
            P(("grp", "inst"), None, "tp", None),
            P(("grp", "inst"), None, "tp", None),
        ),
        out_specs=(
            P(("grp", "inst"), None, "tp", None),
            P(("grp", "inst"), "tp", None, None),
            P(("grp", "inst"), "tp", None, None),
        ),
        check_vma=False,
    )
```

```python
import math

import jax
import jax.numpy as jnp
from jax import lax
from jax.experimental import pallas as pl
from jax.experimental.pallas import tpu as pltpu
from jax.sharding import PartitionSpec as P

masked_score = -1e30


def passed_along(value, axis, steps):
    count = lax.axis_size(axis)
    pairs = [(source, (source + steps) % count) for source in range(count)]
    return lax.ppermute(value, axis, pairs)


def attend_batch(key_blocks, value_blocks, length, query_tokens, recent_keys, recent_values):
    row_count, step_count, head_count, head_width = query_tokens.shape
    kv_count = key_blocks.shape[2]
    group_size = head_count // kv_count
    block_count = key_blocks.shape[1]
    block_len = key_blocks.shape[3]
    score_scale = 1.0 / math.sqrt(head_width)
    grouped = query_tokens.reshape(row_count, step_count, kv_count, group_size, head_width)
    context = (
        jnp.einsum("rsgqd,rbgtd->rsgqbt", grouped, key_blocks, preferred_element_type=jnp.float32)
        * score_scale
    )
    position = (
        jnp.arange(block_count, dtype=jnp.int32)[:, None] * block_len
        + jnp.arange(block_len, dtype=jnp.int32)[None, :]
    )
    valid = position[None] < length[:, None, None]
    context = jnp.where(valid[:, None, None, None], context, masked_score)
    recent = (
        jnp.einsum("rsgqd,rtgd->rsgqt", grouped, recent_keys, preferred_element_type=jnp.float32)
        * score_scale
    )
    causal = jnp.arange(step_count)[None, :] <= jnp.arange(step_count)[:, None]
    recent = jnp.where(causal[None, :, None, None, :], recent, masked_score)
    highest = jnp.maximum(jnp.max(context, axis=(4, 5)), jnp.max(recent, axis=4))
    context_exp = jnp.exp(context - highest[..., None, None])
    recent_exp = jnp.exp(recent - highest[..., None])
    denominator = jnp.sum(context_exp, axis=(4, 5)) + jnp.sum(recent_exp, axis=4)
    context_weight = (context_exp / denominator[..., None, None]).astype(jnp.bfloat16)
    recent_weight = (recent_exp / denominator[..., None]).astype(jnp.bfloat16)
    result_sum = jnp.einsum(
        "rsgqbt,rbgtd->rsgqd", context_weight, value_blocks, preferred_element_type=jnp.float32
    )
    result_sum = result_sum + jnp.einsum(
        "rsgqt,rtgd->rsgqd", recent_weight, recent_values, preferred_element_type=jnp.float32
    )
    return result_sum.astype(jnp.bfloat16).reshape(row_count, step_count, head_count, head_width)


def guest_block(blocks, length, recent_rows):
    block_count, kv_count, block_len, head_width = blocks.shape
    position = (
        jnp.arange(block_count, dtype=jnp.int32)[:, None] * block_len
        + jnp.arange(block_len, dtype=jnp.int32)[None, :]
    )
    position = position[:, None, :, None]
    filled = jnp.where(position < length, blocks, jnp.zeros_like(blocks))
    for step_index in range(recent_rows.shape[0]):
        filled = jnp.where(
            position == length + step_index, recent_rows[step_index][None, :, None, :], filled
        )
    return filled


def pick_kernel(blocks, half_cycle, pairs_ref, table_ref, key_ref, value_ref, keys_out, values_out, sems):
    row = lax.rem(lax.axis_index("inst"), half_cycle)
    request = pairs_ref[row, 1]
    copies = []
    for block in range(blocks):
        place = table_ref[block, request]
        copies.append(pltpu.make_async_copy(key_ref.at[place], keys_out.at[block], sems.at[block]))
        copies.append(
            pltpu.make_async_copy(value_ref.at[place], values_out.at[block], sems.at[blocks + block])
        )
    for copy in copies:
        copy.start()
    for copy in copies:
        copy.wait()


def pick_moved(key_pool, value_pool, block_table, pairs, half_cycle):
    blocks = block_table.shape[1]
    shape = jax.ShapeDtypeStruct((blocks,) + key_pool.shape[1:], key_pool.dtype)
    smem = pl.BlockSpec(memory_space=pltpu.SMEM)
    vmem = pl.BlockSpec(memory_space=pltpu.VMEM)
    pool = pl.BlockSpec(memory_space=pltpu.HBM)
    return pl.pallas_call(
        lambda *refs: pick_kernel(blocks, half_cycle, *refs),
        out_shape=(shape, shape),
        in_specs=[smem, smem, pool, pool],
        out_specs=(vmem, vmem),
        scratch_shapes=[pltpu.SemaphoreType.DMA((2 * blocks,))],
        name="pick_moved",
    )(pairs, block_table.T, key_pool, value_pool)


def shards(
    key_pool,
    value_pool,
    block_table,
    lengths,
    pairs,
    queries,
    new_keys,
    new_values,
    guest_queries,
    guest_new_keys,
    guest_new_values,
):
    half_cycle = lax.axis_size("inst") // 2
    own_index = lax.axis_index("inst")
    send_keys, send_values = pick_moved(key_pool, value_pool, block_table, pairs, half_cycle)
    got_keys = passed_along(send_keys, "inst", half_cycle)
    got_values = passed_along(send_values, "inst", half_cycle)
    guest_tokens = jnp.concatenate([guest_queries, guest_new_keys, guest_new_values], axis=2)
    moved_tokens = passed_along(guest_tokens, "inst", half_cycle)
    head_count = queries.shape[2]
    kv_count = new_keys.shape[2]

    pair_row = lax.dynamic_index_in_dim(pairs, own_index % half_cycle, 0, keepdims=False)
    source = pair_row[0]
    request = pair_row[1]
    target = pair_row[2]
    own_lengths = lax.dynamic_index_in_dim(lengths, own_index, 0, keepdims=False)
    source_lengths = lax.dynamic_index_in_dim(lengths, source, 0, keepdims=False)
    moved_length = lax.dynamic_index_in_dim(source_lengths, request, 0, keepdims=False)
    row_ids = jnp.arange(own_lengths.shape[0], dtype=jnp.int32)
    replace = ((source == own_index) & (row_ids == request))[:, None, None, None]
    attended = attend_batch(
        key_pool[block_table],
        value_pool[block_table],
        own_lengths,
        jnp.where(replace, moved_tokens[:, :, :head_count], queries),
        jnp.where(replace, moved_tokens[:, :, head_count : head_count + kv_count], new_keys),
        jnp.where(replace, moved_tokens[:, :, head_count + kv_count :], new_values),
    )
    receiving = target == own_index
    guest_length = jnp.where(receiving, moved_length, -guest_new_keys.shape[1])
    guest_keys = guest_block(got_keys, guest_length, guest_new_keys[0])
    guest_keys, got_values = lax.optimization_barrier((guest_keys, got_values))
    guest_values = guest_block(got_values, guest_length, guest_new_values[0])
    return (attended, guest_keys, guest_values)


def solution(mesh):
    return jax.shard_map(
        shards,
        mesh=mesh,
        in_specs=(
            P(("grp", "inst"), "tp", None, None),
            P(("grp", "inst"), "tp", None, None),
            P(("grp", "inst"), None),
            P("grp", None),
            P("grp", None),
            P(("grp", "inst"), None, "tp", None),
            P(("grp", "inst"), None, "tp", None),
            P(("grp", "inst"), None, "tp", None),
            P(("grp", "inst"), None, "tp", None),
            P(("grp", "inst"), None, "tp", None),
            P(("grp", "inst"), None, "tp", None),
        ),
        out_specs=(
            P(("grp", "inst"), None, "tp", None),
            P(("grp", "inst"), "tp", None, None),
            P(("grp", "inst"), "tp", None, None),
        ),
        check_vma=False,
    )
```

```python
import math

import jax
import jax.numpy as jnp
from jax import lax
from jax.experimental import pallas as pl
from jax.experimental.pallas import tpu as pltpu
from jax.sharding import PartitionSpec as P

masked_score = -1e30


def passed_along(value, axis, steps):
    count = lax.axis_size(axis)
    pairs = [(source, (source + steps) % count) for source in range(count)]
    return lax.ppermute(value, axis, pairs)


def attend_kernel(
    lengths_ref, table_ref, key_ref, value_ref, query_ref, recent_key_ref, recent_value_ref, out_ref,
    keys, values, recent_scores, sems,
):
    kv_count, block_len, head_width = key_ref.shape[1:]
    block_count, row_count = table_ref.shape
    token_rows = query_ref.shape[1] // row_count
    step_count = recent_key_ref.shape[1] // row_count
    group_size = token_rows // step_count
    score_scale = 1.0 / math.sqrt(head_width)
    own_index = lax.axis_index("inst")

    def copies(row, block):
        place = table_ref[block, row]
        return (
            pltpu.make_async_copy(key_ref.at[place], keys.at[place], sems.at[0, block, row]),
            pltpu.make_async_copy(value_ref.at[place], values.at[place], sems.at[1, block, row]),
        )

    @pl.loop(0, row_count)
    def _(row):
        for block in range(block_count):

            @pl.when(block * block_len < lengths_ref[own_index, row])
            def _():
                for copy in copies(row, block):
                    copy.start()

    contract_last = (((1,), (1,)), ((), ()))
    rows = lax.broadcasted_iota(jnp.int32, recent_scores.shape[1:], 0)
    columns = lax.broadcasted_iota(jnp.int32, recent_scores.shape[1:], 1)
    step = (rows % token_rows) // group_size
    seen = (rows // token_rows == columns // step_count) & (columns % step_count <= step)
    for head in range(kv_count):
        products = lax.dot_general(
            query_ref[head], recent_key_ref[head], contract_last, preferred_element_type=jnp.float32
        )
        recent_scores[head] = jnp.where(seen, products * score_scale, masked_score)

    @pl.loop(0, row_count)
    def _(row):
        length = lengths_ref[own_index, row]
        own_rows = pl.ds(pl.multiple_of(row * token_rows, token_rows), token_rows)

        def attend(used):
            places = [table_ref[block, row] for block in range(used)]
            for block in range(used):
                for copy in copies(row, block):
                    copy.wait()
            for head in range(kv_count):
                query = query_ref[head, own_rows, :]
                scores = []
                for block in range(used):
                    products = lax.dot_general(
                        query,
                        keys[places[block], head],
                        contract_last,
                        preferred_element_type=jnp.float32,
                    )
                    scores.append(products * score_scale)
                position = lax.broadcasted_iota(jnp.int32, scores[-1].shape, 1) + (used - 1) * block_len
                scores[-1] = jnp.where(position < length, scores[-1], masked_score)
                scores = jnp.concatenate(scores, axis=1)
                recent = recent_scores[head, own_rows, :]
                highest = jnp.maximum(
                    jnp.max(scores, axis=1, keepdims=True), jnp.max(recent, axis=1, keepdims=True)
                )
                weight = jnp.exp(scores - highest)
                recent_weight = jnp.exp(recent - highest)
                denominator = jnp.sum(weight, axis=1, keepdims=True) + jnp.sum(
                    recent_weight, axis=1, keepdims=True
                )
                weight = (weight / denominator).astype(jnp.bfloat16)
                recent_weight = (recent_weight / denominator).astype(jnp.bfloat16)
                total = jnp.dot(
                    recent_weight, recent_value_ref[head], preferred_element_type=jnp.float32
                )
                for block in range(used):
                    total += jnp.dot(
                        weight[:, block * block_len : (block + 1) * block_len],
                        values[places[block], head],
                        preferred_element_type=jnp.float32,
                    )
                out_ref[head, own_rows, :] = total.astype(out_ref.dtype)

        for used in range(1, block_count + 1):
            pl.when((length + block_len - 1) // block_len == used)(lambda used=used: attend(used))


def attend_rows(key_pool, value_pool, block_table, lengths, query_tokens, recent_keys, recent_values):
    row_count, step_count, head_count, head_width = query_tokens.shape
    kv_count = key_pool.shape[1]
    group_size = head_count // kv_count
    block_count = block_table.shape[1]
    grouped = query_tokens.reshape(row_count, step_count, kv_count, group_size, head_width)
    grouped = grouped.transpose(2, 0, 1, 3, 4).reshape(kv_count, -1, head_width)
    recent_keys = recent_keys.transpose(2, 0, 1, 3).reshape(kv_count, -1, head_width)
    recent_values = recent_values.transpose(2, 0, 1, 3).reshape(kv_count, -1, head_width)
    smem = pl.BlockSpec(memory_space=pltpu.SMEM)
    vmem = pl.BlockSpec(memory_space=pltpu.VMEM)
    pool = pl.BlockSpec(memory_space=pltpu.HBM)
    out = pl.pallas_call(
        attend_kernel,
        out_shape=jax.ShapeDtypeStruct(grouped.shape, grouped.dtype),
        in_specs=[smem, smem, pool, pool, vmem, vmem, vmem],
        out_specs=vmem,
        scratch_shapes=[
            pltpu.VMEM(key_pool.shape, key_pool.dtype),
            pltpu.VMEM(value_pool.shape, value_pool.dtype),
            pltpu.VMEM(grouped.shape[:2] + recent_keys.shape[1:2], jnp.float32),
            pltpu.SemaphoreType.DMA((2, block_count, row_count)),
        ],
        compiler_params=pltpu.CompilerParams(vmem_limit_bytes=24 * 1024 * 1024),
        cost_estimate=pl.CostEstimate(
            flops=4 * grouped.size * block_count * key_pool.shape[2],
            bytes_accessed=2 * key_pool.size * 2,
            transcendentals=grouped.size * block_count,
        ),
        name="attend",
    )(lengths, block_table.T, key_pool, value_pool, grouped, recent_keys, recent_values)
    out = out.reshape(kv_count, row_count, step_count, group_size, head_width)
    return out.transpose(1, 2, 0, 3, 4).reshape(query_tokens.shape)


def guest_block(blocks, length, recent_rows):
    block_count, kv_count, block_len, head_width = blocks.shape
    position = (
        jnp.arange(block_count, dtype=jnp.int32)[:, None] * block_len
        + jnp.arange(block_len, dtype=jnp.int32)[None, :]
    )
    position = position[:, None, :, None]
    filled = jnp.where(position < length, blocks, jnp.zeros_like(blocks))
    for step_index in range(recent_rows.shape[0]):
        filled = jnp.where(
            position == length + step_index, recent_rows[step_index][None, :, None, :], filled
        )
    return filled


def pick_kernel(blocks, half_cycle, pairs_ref, table_ref, key_ref, value_ref, keys_out, values_out, sems):
    row = lax.rem(lax.axis_index("inst"), half_cycle)
    request = pairs_ref[row, 1]
    copies = []
    for block in range(blocks):
        place = table_ref[block, request]
        copies.append(pltpu.make_async_copy(key_ref.at[place], keys_out.at[block], sems.at[block]))
        copies.append(
            pltpu.make_async_copy(value_ref.at[place], values_out.at[block], sems.at[blocks + block])
        )
    for copy in copies:
        copy.start()
    for copy in copies:
        copy.wait()


def pick_moved(key_pool, value_pool, block_table, pairs, half_cycle):
    blocks = block_table.shape[1]
    shape = jax.ShapeDtypeStruct((blocks,) + key_pool.shape[1:], key_pool.dtype)
    smem = pl.BlockSpec(memory_space=pltpu.SMEM)
    vmem = pl.BlockSpec(memory_space=pltpu.VMEM)
    pool = pl.BlockSpec(memory_space=pltpu.HBM)
    return pl.pallas_call(
        lambda *refs: pick_kernel(blocks, half_cycle, *refs),
        out_shape=(shape, shape),
        in_specs=[smem, smem, pool, pool],
        out_specs=(vmem, vmem),
        scratch_shapes=[pltpu.SemaphoreType.DMA((2 * blocks,))],
        name="pick_moved",
    )(pairs, block_table.T, key_pool, value_pool)


def shards(
    key_pool,
    value_pool,
    block_table,
    lengths,
    pairs,
    queries,
    new_keys,
    new_values,
    guest_queries,
    guest_new_keys,
    guest_new_values,
):
    half_cycle = lax.axis_size("inst") // 2
    own_index = lax.axis_index("inst")
    send_keys, send_values = pick_moved(key_pool, value_pool, block_table, pairs, half_cycle)
    got_keys = passed_along(send_keys, "inst", half_cycle)
    got_values = passed_along(send_values, "inst", half_cycle)
    guest_tokens = jnp.concatenate([guest_queries, guest_new_keys, guest_new_values], axis=2)
    guest_tokens, send_keys = lax.optimization_barrier((guest_tokens, send_keys))
    moved_tokens = passed_along(guest_tokens, "inst", half_cycle)
    head_count = queries.shape[2]
    kv_count = new_keys.shape[2]

    pair_row = lax.dynamic_index_in_dim(pairs, own_index % half_cycle, 0, keepdims=False)
    source = pair_row[0]
    request = pair_row[1]
    target = pair_row[2]
    own_lengths = lax.dynamic_index_in_dim(lengths, own_index, 0, keepdims=False)
    source_lengths = lax.dynamic_index_in_dim(lengths, source, 0, keepdims=False)
    moved_length = lax.dynamic_index_in_dim(source_lengths, request, 0, keepdims=False)
    row_ids = jnp.arange(own_lengths.shape[0], dtype=jnp.int32)
    replace = ((source == own_index) & (row_ids == request))[:, None, None, None]
    attended = attend_rows(
        key_pool,
        value_pool,
        block_table,
        lengths,
        jnp.where(replace, moved_tokens[:, :, :head_count], queries),
        jnp.where(replace, moved_tokens[:, :, head_count : head_count + kv_count], new_keys),
        jnp.where(replace, moved_tokens[:, :, head_count + kv_count :], new_values),
    )
    receiving = target == own_index
    guest_length = jnp.where(receiving, moved_length, -guest_new_keys.shape[1])
    guest_keys = guest_block(got_keys, guest_length, guest_new_keys[0])
    guest_keys, got_values = lax.optimization_barrier((guest_keys, got_values))
    guest_values = guest_block(got_values, guest_length, guest_new_values[0])
    return (attended, guest_keys, guest_values)


def solution(mesh):
    return jax.shard_map(
        shards,
        mesh=mesh,
        in_specs=(
            P(("grp", "inst"), "tp", None, None),
            P(("grp", "inst"), "tp", None, None),
            P(("grp", "inst"), None),
            P("grp", None),
            P("grp", None),
            P(("grp", "inst"), None, "tp", None),
            P(("grp", "inst"), None, "tp", None),
            P(("grp", "inst"), None, "tp", None),
            P(("grp", "inst"), None, "tp", None),
            P(("grp", "inst"), None, "tp", None),
            P(("grp", "inst"), None, "tp", None),
        ),
        out_specs=(
            P(("grp", "inst"), None, "tp", None),
            P(("grp", "inst"), "tp", None, None),
            P(("grp", "inst"), "tp", None, None),
        ),
        check_vma=False,
    )
```

```python
import functools
import math

import jax
import jax.numpy as jnp
from jax import lax
from jax.experimental import pallas as pl
from jax.experimental.pallas import tpu as pltpu
from jax.sharding import PartitionSpec as P

masked_score = -1e30


def passed_along(value, axis, steps):
    count = lax.axis_size(axis)
    pairs = [(source, (source + steps) % count) for source in range(count)]
    return lax.ppermute(value, axis, pairs)


def attend_kernel(
    lengths_ref, table_ref, pairs_ref, key_ref, value_ref, query_ref, recent_key_ref, recent_value_ref,
    moved_ref, out_ref,
):
    kv_count, block_len, head_width = key_ref.shape[1:]
    block_count, row_count = table_ref.shape
    step_count, head_count = query_ref.shape[1:3]
    group_size = head_count // kv_count
    token_rows = step_count * group_size
    score_scale = 1.0 / math.sqrt(head_width)
    contract_last = (((1,), (1,)), ((), ()))
    heads = range(kv_count)
    own_index = lax.axis_index("inst")
    pair = lax.rem(own_index, pairs_ref.shape[0])
    moved_row = jnp.where(pairs_ref[pair, 0] == own_index, pairs_ref[pair, 1], -1)

    def by_head(query):
        query = query.astype(jnp.float32).reshape(step_count, kv_count, group_size, head_width)
        return query.transpose(1, 0, 2, 3).reshape(kv_count * token_rows, head_width)

    def by_step(recent):
        recent = recent.astype(jnp.float32)
        return jnp.concatenate([recent[step] for step in range(step_count)], axis=0)

    moved_query = by_head(moved_ref[0, :, :head_count, :])
    moved_key = by_step(moved_ref[0, :, head_count : head_count + kv_count, :])
    moved_value = by_step(moved_ref[0, :, head_count + kv_count :, :])
    recent_shape = (kv_count * token_rows, step_count * kv_count)
    rows = lax.broadcasted_iota(jnp.int32, recent_shape, 0)
    columns = lax.broadcasted_iota(jnp.int32, recent_shape, 1)
    seen = (rows // token_rows == columns % kv_count) & (
        columns // kv_count <= (rows % token_rows) // group_size
    )

    @pl.loop(0, row_count)
    def _(row):
        length = lengths_ref[own_index, row]
        moved = row == moved_row
        query = jnp.where(moved, moved_query, by_head(query_ref[row])).astype(jnp.bfloat16)
        recent_key = jnp.where(moved, moved_key, by_step(recent_key_ref[row])).astype(jnp.bfloat16)
        recent_value = jnp.where(moved, moved_value, by_step(recent_value_ref[row]))
        recent = lax.dot_general(query, recent_key, contract_last, preferred_element_type=jnp.float32)
        recent = jnp.where(seen, recent * score_scale, masked_score)
        recent_value = recent_value.astype(jnp.bfloat16)

        def attend(used):
            places = [table_ref[block, row] for block in range(used)]
            scores = []
            for block in range(used):
                products = [
                    lax.dot_general(
                        query[head * token_rows : (head + 1) * token_rows],
                        key_ref[places[block], head],
                        contract_last,
                        preferred_element_type=jnp.float32,
                    )
                    for head in heads
                ]
                scores.append(jnp.concatenate(products, axis=0) * score_scale)
            position = lax.broadcasted_iota(jnp.int32, scores[-1].shape, 1) + (used - 1) * block_len
            scores[-1] = jnp.where(position < length, scores[-1], masked_score)
            highest = functools.reduce(jnp.maximum, scores)
            highest = jnp.maximum(
                jnp.max(highest, axis=1, keepdims=True), jnp.max(recent, axis=1, keepdims=True)
            )
            weights = [jnp.exp(score - highest) for score in scores]
            recent_weight = jnp.exp(recent - highest)
            denominator = jnp.sum(functools.reduce(jnp.add, weights), axis=1, keepdims=True)
            denominator += jnp.sum(recent_weight, axis=1, keepdims=True)
            scale = 1.0 / denominator
            weights = [(weight * scale).astype(jnp.bfloat16) for weight in weights]
            recent_weight = (recent_weight * scale).astype(jnp.bfloat16)
            total = jnp.dot(recent_weight, recent_value, preferred_element_type=jnp.float32)
            sums = []
            for head in heads:
                own = slice(head * token_rows, (head + 1) * token_rows)
                part = total[own]
                for block in range(used):
                    part += jnp.dot(
                        weights[block][own],
                        value_ref[places[block], head],
                        preferred_element_type=jnp.float32,
                    )
                sums.append(part)
            total = jnp.concatenate(sums, axis=0)
            total = total.reshape(kv_count, step_count, group_size, head_width)
            total = total.transpose(1, 0, 2, 3).reshape(step_count, head_count, head_width)
            out_ref[row] = total.astype(out_ref.dtype)

        for used in range(1, block_count + 1):
            pl.when((length + block_len - 1) // block_len == used)(functools.partial(attend, used))


def attend_rows(
    key_pool, value_pool, block_table, lengths, pairs, queries, recent_keys, recent_values, moved_tokens
):
    block_count = block_table.shape[1]
    smem = pl.BlockSpec(memory_space=pltpu.SMEM)
    vmem = pl.BlockSpec(memory_space=pltpu.VMEM)
    return pl.pallas_call(
        attend_kernel,
        out_shape=jax.ShapeDtypeStruct(queries.shape, queries.dtype),
        in_specs=[smem, smem, smem, vmem, vmem, vmem, vmem, vmem, vmem],
        out_specs=vmem,
        compiler_params=pltpu.CompilerParams(vmem_limit_bytes=24 * 1024 * 1024),
        cost_estimate=pl.CostEstimate(flops=1, bytes_accessed=1, transcendentals=1),
        name="attend",
    )(
        lengths, block_table.T, pairs, key_pool, value_pool, queries, recent_keys, recent_values,
        moved_tokens,
    )


def guest_block(blocks, length, recent_rows):
    block_count, kv_count, block_len, head_width = blocks.shape
    position = (
        jnp.arange(block_count, dtype=jnp.int32)[:, None] * block_len
        + jnp.arange(block_len, dtype=jnp.int32)[None, :]
    )
    position = position[:, None, :, None]
    filled = jnp.where(position < length, blocks, jnp.zeros_like(blocks))
    for step_index in range(recent_rows.shape[0]):
        filled = jnp.where(
            position == length + step_index, recent_rows[step_index][None, :, None, :], filled
        )
    return filled


def pick_kernel(
    half_cycle, step_count, pairs_ref, table_ref, lengths_ref, key_ref, value_ref,
    facts_out, keys_out, values_out, sems,
):
    own_index = lax.axis_index("inst")
    row = lax.rem(own_index, half_cycle)
    request = pairs_ref[row, 1]
    blocks = table_ref.shape[0]
    copies = []
    for block in range(blocks):
        place = table_ref[block, request]
        copies.append(pltpu.make_async_copy(key_ref.at[place], keys_out.at[block], sems.at[block]))
        copies.append(
            pltpu.make_async_copy(value_ref.at[place], values_out.at[block], sems.at[blocks + block])
        )
    for copy in copies:
        copy.start()
    first = row - lax.rem(row, 2)
    second = jnp.minimum(first + 1, half_cycle - 1)
    facts_out[0] = (pairs_ref[first, 0] >= half_cycle).astype(jnp.int32) + 2 * (
        pairs_ref[second, 0] >= half_cycle
    ).astype(jnp.int32)
    moved_length = lengths_ref[pairs_ref[row, 0], request]
    facts_out[1] = jnp.where(pairs_ref[row, 2] == own_index, moved_length, -step_count)
    for copy in copies:
        copy.wait()


def pick_moved(key_pool, value_pool, block_table, lengths, pairs, half_cycle, step_count):
    blocks = block_table.shape[1]
    shape = jax.ShapeDtypeStruct((blocks,) + key_pool.shape[1:], key_pool.dtype)
    smem = pl.BlockSpec(memory_space=pltpu.SMEM)
    vmem = pl.BlockSpec(memory_space=pltpu.VMEM)
    pool = pl.BlockSpec(memory_space=pltpu.HBM)
    return pl.pallas_call(
        functools.partial(pick_kernel, half_cycle, step_count),
        out_shape=(jax.ShapeDtypeStruct((2,), jnp.int32), shape, shape),
        in_specs=[smem, smem, smem, pool, pool],
        out_specs=(smem, vmem, vmem),
        scratch_shapes=[pltpu.SemaphoreType.DMA((2 * blocks,))],
        name="pick_moved",
    )(pairs, block_table.T, lengths, key_pool, value_pool)


def plan_of(pattern, half_cycle):
    straight, to_neighbour, from_neighbour = [], [], []
    for low in range(half_cycle):
        ends = (low, low + half_cycle)
        source, target = ends[::-1] if pattern >> (low % 2) & 1 else ends
        straight.append((source, target))
        to_neighbour.append((source, source ^ 1))
        from_neighbour.append((source ^ 1, target))
    return straight, to_neighbour, from_neighbour


def shards(
    key_pool,
    value_pool,
    block_table,
    lengths,
    pairs,
    queries,
    new_keys,
    new_values,
    guest_queries,
    guest_new_keys,
    guest_new_values,
    *,
    relayed,
):
    half_cycle = lax.axis_size("inst") // 2
    step_count = queries.shape[1]
    guest_tokens = jnp.concatenate([guest_queries, guest_new_keys, guest_new_values], axis=2)
    moved_tokens = passed_along(guest_tokens, "inst", half_cycle)
    facts, send_keys, send_values = pick_moved(
        key_pool, value_pool, block_table, lengths, pairs, half_cycle, step_count
    )

    def finish(send, operands):
        (
            key_pool, value_pool, block_table, lengths, pairs, queries, new_keys, new_values,
            moved_tokens, guest_new_keys, guest_new_values, facts, send_keys, send_values,
        ) = operands
        got_keys, got_values = send(send_keys, send_values)
        attended = attend_rows(
            key_pool, value_pool, block_table, lengths, pairs, queries, new_keys, new_values, moved_tokens
        )
        guest_length = facts[1]
        guest_keys = guest_block(got_keys, guest_length, guest_new_keys[0])
        guest_keys, got_values = lax.optimization_barrier((guest_keys, got_values))
        guest_values = guest_block(got_values, guest_length, guest_new_values[0])
        return (attended, guest_keys, guest_values)

    def send_both_ways(*arrays):
        return [passed_along(array, "inst", half_cycle) for array in arrays]

    def send_one_way(pattern, keys, values):
        straight, to_neighbour, from_neighbour = plan_of(pattern, half_cycle)
        got_keys = lax.ppermute(keys, "inst", straight)
        if pattern in (0, 3):
            return got_keys, lax.ppermute(values, "inst", straight)
        half = values.shape[0] // 2
        parts = []
        for part in (values[:half], values[half:]):
            relayed = lax.ppermute(part, "inst", to_neighbour)
            parts.append(lax.ppermute(relayed, "inst", from_neighbour))
        return got_keys, jnp.concatenate(parts, axis=0)

    operands = (
        key_pool, value_pool, block_table, lengths, pairs, queries, new_keys, new_values,
        moved_tokens, guest_new_keys, guest_new_values, facts, send_keys, send_values,
    )
    if not relayed:
        return finish(send_both_ways, operands)
    branches = [
        functools.partial(finish, functools.partial(send_one_way, pattern)) for pattern in range(4)
    ]
    return lax.switch(facts[0], branches, operands)


def solution(mesh):
    relayed = mesh.shape["inst"] == 8
    return jax.shard_map(
        functools.partial(shards, relayed=relayed),
        mesh=mesh,
        in_specs=(
            P(("grp", "inst"), "tp", None, None),
            P(("grp", "inst"), "tp", None, None),
            P(("grp", "inst"), None),
            P("grp", None),
            P("grp", None),
            P(("grp", "inst"), None, "tp", None),
            P(("grp", "inst"), None, "tp", None),
            P(("grp", "inst"), None, "tp", None),
            P(("grp", "inst"), None, "tp", None),
            P(("grp", "inst"), None, "tp", None),
            P(("grp", "inst"), None, "tp", None),
        ),
        out_specs=(
            P(("grp", "inst"), None, "tp", None),
            P(("grp", "inst"), "tp", None, None),
            P(("grp", "inst"), "tp", None, None),
        ),
        check_vma=False,
    )
```

```python
import functools
import math

import jax
import jax.numpy as jnp
from jax import lax
from jax.experimental import pallas as pl
from jax.experimental.pallas import tpu as pltpu
from jax.sharding import PartitionSpec as P

masked_score = -1e30


def passed_along(value, axis, steps):
    count = lax.axis_size(axis)
    pairs = [(source, (source + steps) % count) for source in range(count)]
    return lax.ppermute(value, axis, pairs)


def attend_kernel(
    lengths_ref, table_ref, pairs_ref, key_ref, value_ref, query_ref, recent_key_ref, recent_value_ref,
    moved_ref, out_ref,
):
    kv_count, block_len, head_width = key_ref.shape[1:]
    block_count, row_count = table_ref.shape
    step_count, head_count = query_ref.shape[1:3]
    group_size = head_count // kv_count
    token_rows = step_count * group_size
    score_scale = 1.0 / math.sqrt(head_width)
    contract_last = (((1,), (1,)), ((), ()))
    heads = range(kv_count)
    own_index = lax.axis_index("inst")
    pair = lax.rem(own_index, pairs_ref.shape[0])
    moved_row = jnp.where(pairs_ref[pair, 0] == own_index, pairs_ref[pair, 1], -1)

    def by_head(query):
        query = query.astype(jnp.float32).reshape(step_count, kv_count, group_size, head_width)
        return query.transpose(1, 0, 2, 3).reshape(kv_count * token_rows, head_width)

    def by_step(recent):
        recent = recent.astype(jnp.float32)
        return jnp.concatenate([recent[step] for step in range(step_count)], axis=0)

    moved_query = by_head(moved_ref[0, :, :head_count, :])
    moved_key = by_step(moved_ref[0, :, head_count : head_count + kv_count, :])
    moved_value = by_step(moved_ref[0, :, head_count + kv_count :, :])
    recent_shape = (kv_count * token_rows, step_count * kv_count)
    token = lax.broadcasted_iota(jnp.int32, recent_shape, 0)
    columns = lax.broadcasted_iota(jnp.int32, recent_shape, 1)
    seen = (token // token_rows == columns % kv_count) & (
        columns // kv_count <= (token % token_rows) // group_size
    )

    own_rows = kv_count * token_rows
    together = math.gcd(row_count, 2)

    @pl.loop(0, row_count // together)
    def _(first):
        rows = [first * together + member for member in range(together)]
        members = range(together)
        lengths = [lengths_ref[own_index, row] for row in rows]
        queries, recent_values, recent = [], [], []
        for row in rows:
            moved = row == moved_row
            query = jnp.where(moved, moved_query, by_head(query_ref[row])).astype(jnp.bfloat16)
            recent_key = jnp.where(moved, moved_key, by_step(recent_key_ref[row]))
            recent_value = jnp.where(moved, moved_value, by_step(recent_value_ref[row]))
            queries.append(query)
            recent_values.append(recent_value.astype(jnp.bfloat16))
            products = lax.dot_general(
                query,
                recent_key.astype(jnp.bfloat16),
                contract_last,
                preferred_element_type=jnp.float32,
            )
            recent.append(jnp.where(seen, products * score_scale, masked_score))
        recent = jnp.concatenate(recent, axis=0)

        def attend(used):
            places = [[table_ref[block, row] for block in range(used)] for row in rows]
            shape = (own_rows, block_len)
            length = jnp.concatenate([jnp.full(shape, own, jnp.int32) for own in lengths], axis=0)
            position = lax.broadcasted_iota(jnp.int32, length.shape, 1)
            scores = []
            for block in range(used):
                products = [
                    lax.dot_general(
                        queries[member][head * token_rows : (head + 1) * token_rows],
                        key_ref[places[member][block], head],
                        contract_last,
                        preferred_element_type=jnp.float32,
                    )
                    for member in members
                    for head in heads
                ]
                products = jnp.concatenate(products, axis=0) * score_scale
                here = position + block * block_len < length
                scores.append(jnp.where(here, products, masked_score))
            highest = functools.reduce(jnp.maximum, scores)
            highest = jnp.maximum(
                jnp.max(highest, axis=1, keepdims=True), jnp.max(recent, axis=1, keepdims=True)
            )
            weights = [jnp.exp(score - highest) for score in scores]
            recent_weight = jnp.exp(recent - highest)
            denominator = jnp.sum(functools.reduce(jnp.add, weights), axis=1, keepdims=True)
            denominator += jnp.sum(recent_weight, axis=1, keepdims=True)
            scale = 1.0 / denominator
            weights = [(weight * scale).astype(jnp.bfloat16) for weight in weights]
            recent_weight = (recent_weight * scale).astype(jnp.bfloat16)
            for member in members:
                start = member * own_rows
                total = jnp.dot(
                    recent_weight[start : start + own_rows],
                    recent_values[member],
                    preferred_element_type=jnp.float32,
                )
                sums = []
                for head in heads:
                    own = slice(head * token_rows, (head + 1) * token_rows)
                    part = total[own]
                    for block in range(used):
                        part += jnp.dot(
                            weights[block][start + own.start : start + own.stop],
                            value_ref[places[member][block], head],
                            preferred_element_type=jnp.float32,
                        )
                    sums.append(part)
                total = jnp.concatenate(sums, axis=0)
                total = total.reshape(kv_count, step_count, group_size, head_width)
                total = total.transpose(1, 0, 2, 3).reshape(step_count, head_count, head_width)
                out_ref[rows[member]] = total.astype(out_ref.dtype)

        longest = functools.reduce(jnp.maximum, lengths)
        for used in range(1, block_count + 1):
            pl.when((longest + block_len - 1) // block_len == used)(functools.partial(attend, used))


def attend_rows(
    key_pool, value_pool, block_table, lengths, pairs, queries, recent_keys, recent_values, moved_tokens
):
    block_count = block_table.shape[1]
    smem = pl.BlockSpec(memory_space=pltpu.SMEM)
    vmem = pl.BlockSpec(memory_space=pltpu.VMEM)
    return pl.pallas_call(
        attend_kernel,
        out_shape=jax.ShapeDtypeStruct(queries.shape, queries.dtype),
        in_specs=[smem, smem, smem, vmem, vmem, vmem, vmem, vmem, vmem],
        out_specs=vmem,
        compiler_params=pltpu.CompilerParams(vmem_limit_bytes=24 * 1024 * 1024),
        cost_estimate=pl.CostEstimate(flops=1, bytes_accessed=1, transcendentals=1),
        name="attend",
    )(
        lengths, block_table.T, pairs, key_pool, value_pool, queries, recent_keys, recent_values,
        moved_tokens,
    )


def guest_block(blocks, length, recent_rows):
    block_count, kv_count, block_len, head_width = blocks.shape
    position = (
        jnp.arange(block_count, dtype=jnp.int32)[:, None] * block_len
        + jnp.arange(block_len, dtype=jnp.int32)[None, :]
    )
    position = position[:, None, :, None]
    filled = jnp.where(position < length, blocks, jnp.zeros_like(blocks))
    for step_index in range(recent_rows.shape[0]):
        filled = jnp.where(
            position == length + step_index, recent_rows[step_index][None, :, None, :], filled
        )
    return filled


def pick_kernel(
    half_cycle, step_count, pairs_ref, table_ref, lengths_ref, key_ref, value_ref,
    facts_out, keys_out, values_out, sems,
):
    own_index = lax.axis_index("inst")
    row = lax.rem(own_index, half_cycle)
    request = pairs_ref[row, 1]
    blocks = table_ref.shape[0]
    copies = []
    for block in range(blocks):
        place = table_ref[block, request]
        copies.append(pltpu.make_async_copy(key_ref.at[place], keys_out.at[block], sems.at[block]))
        copies.append(
            pltpu.make_async_copy(value_ref.at[place], values_out.at[block], sems.at[blocks + block])
        )
    for copy in copies:
        copy.start()
    first = row - lax.rem(row, 2)
    second = jnp.minimum(first + 1, half_cycle - 1)
    facts_out[0] = (pairs_ref[first, 0] >= half_cycle).astype(jnp.int32) + 2 * (
        pairs_ref[second, 0] >= half_cycle
    ).astype(jnp.int32)
    moved_length = lengths_ref[pairs_ref[row, 0], request]
    facts_out[1] = jnp.where(pairs_ref[row, 2] == own_index, moved_length, -step_count)
    for copy in copies:
        copy.wait()


def pick_moved(key_pool, value_pool, block_table, lengths, pairs, half_cycle, step_count):
    blocks = block_table.shape[1]
    shape = jax.ShapeDtypeStruct((blocks,) + key_pool.shape[1:], key_pool.dtype)
    smem = pl.BlockSpec(memory_space=pltpu.SMEM)
    vmem = pl.BlockSpec(memory_space=pltpu.VMEM)
    pool = pl.BlockSpec(memory_space=pltpu.HBM)
    return pl.pallas_call(
        functools.partial(pick_kernel, half_cycle, step_count),
        out_shape=(jax.ShapeDtypeStruct((2,), jnp.int32), shape, shape),
        in_specs=[smem, smem, smem, pool, pool],
        out_specs=(smem, vmem, vmem),
        scratch_shapes=[pltpu.SemaphoreType.DMA((2 * blocks,))],
        name="pick_moved",
    )(pairs, block_table.T, lengths, key_pool, value_pool)


def plan_of(pattern, half_cycle):
    straight, to_neighbour, from_neighbour = [], [], []
    for low in range(half_cycle):
        ends = (low, low + half_cycle)
        source, target = ends[::-1] if pattern >> (low % 2) & 1 else ends
        straight.append((source, target))
        to_neighbour.append((source, source ^ 1))
        from_neighbour.append((source ^ 1, target))
    return straight, to_neighbour, from_neighbour


def shards(
    key_pool,
    value_pool,
    block_table,
    lengths,
    pairs,
    queries,
    new_keys,
    new_values,
    guest_queries,
    guest_new_keys,
    guest_new_values,
    *,
    relayed,
):
    half_cycle = lax.axis_size("inst") // 2
    step_count = queries.shape[1]
    guest_tokens = jnp.concatenate([guest_queries, guest_new_keys, guest_new_values], axis=2)
    moved_tokens = passed_along(guest_tokens, "inst", half_cycle)
    facts, send_keys, send_values = pick_moved(
        key_pool, value_pool, block_table, lengths, pairs, half_cycle, step_count
    )

    def finish(send, operands):
        (
            key_pool, value_pool, block_table, lengths, pairs, queries, new_keys, new_values,
            moved_tokens, guest_new_keys, guest_new_values, facts, send_keys, send_values,
        ) = operands
        got_keys, got_values = send(send_keys, send_values)
        attended = attend_rows(
            key_pool, value_pool, block_table, lengths, pairs, queries, new_keys, new_values, moved_tokens
        )
        guest_length = facts[1]
        guest_keys = guest_block(got_keys, guest_length, guest_new_keys[0])
        guest_keys, *got_values = lax.optimization_barrier((guest_keys, *got_values))
        got_values = got_values[0] if len(got_values) == 1 else jnp.concatenate(got_values, axis=0)
        guest_values = guest_block(got_values, guest_length, guest_new_values[0])
        return (attended, guest_keys, guest_values)

    def send_both_ways(*arrays):
        got_keys, got_values = (passed_along(array, "inst", half_cycle) for array in arrays)
        return got_keys, [got_values]

    def send_one_way(pattern, keys, values):
        straight, to_neighbour, from_neighbour = plan_of(pattern, half_cycle)
        got_keys = lax.ppermute(keys, "inst", straight)
        if pattern in (0, 3):
            return got_keys, [lax.ppermute(values, "inst", straight)]
        half = values.shape[0] // 2
        parts = []
        for part in (values[:half], values[half:]):
            relayed = lax.ppermute(part, "inst", to_neighbour)
            parts.append(lax.ppermute(relayed, "inst", from_neighbour))
        return got_keys, parts

    operands = (
        key_pool, value_pool, block_table, lengths, pairs, queries, new_keys, new_values,
        moved_tokens, guest_new_keys, guest_new_values, facts, send_keys, send_values,
    )
    if not relayed:
        return finish(send_both_ways, operands)
    branches = [
        functools.partial(finish, functools.partial(send_one_way, pattern)) for pattern in range(4)
    ]
    return lax.switch(facts[0], branches, operands)


def solution(mesh):
    relayed = mesh.shape["inst"] == 8
    return jax.shard_map(
        functools.partial(shards, relayed=relayed),
        mesh=mesh,
        in_specs=(
            P(("grp", "inst"), "tp", None, None),
            P(("grp", "inst"), "tp", None, None),
            P(("grp", "inst"), None),
            P("grp", None),
            P("grp", None),
            P(("grp", "inst"), None, "tp", None),
            P(("grp", "inst"), None, "tp", None),
            P(("grp", "inst"), None, "tp", None),
            P(("grp", "inst"), None, "tp", None),
            P(("grp", "inst"), None, "tp", None),
            P(("grp", "inst"), None, "tp", None),
        ),
        out_specs=(
            P(("grp", "inst"), None, "tp", None),
            P(("grp", "inst"), "tp", None, None),
            P(("grp", "inst"), "tp", None, None),
        ),
        check_vma=False,
    )
```

```python
import functools
import math

import jax
import jax.numpy as jnp
from jax import lax
from jax.experimental import pallas as pl
from jax.experimental.pallas import tpu as pltpu
from jax.sharding import PartitionSpec as P

masked_score = -1e30


def passed_along(value, axis, steps):
    count = lax.axis_size(axis)
    pairs = [(source, (source + steps) % count) for source in range(count)]
    return lax.ppermute(value, axis, pairs)


def attend_kernel(
    lengths_ref, table_ref, pairs_ref, key_ref, value_ref, query_ref, recent_key_ref, recent_value_ref,
    moved_ref, out_ref,
):
    kv_count, block_len, head_width = key_ref.shape[1:]
    block_count, row_count = table_ref.shape
    step_count, head_count = query_ref.shape[1:3]
    group_size = head_count // kv_count
    token_rows = step_count * group_size
    score_scale = 1.0 / math.sqrt(head_width)
    contract_last = (((1,), (1,)), ((), ()))
    heads = range(kv_count)
    own_index = lax.axis_index("inst")
    pair = lax.rem(own_index, pairs_ref.shape[0])
    moved_row = jnp.where(pairs_ref[pair, 0] == own_index, pairs_ref[pair, 1], -1)

    def by_head(query):
        query = query.astype(jnp.float32).reshape(step_count, kv_count, group_size, head_width)
        return query.transpose(1, 0, 2, 3).reshape(kv_count * token_rows, head_width)

    def by_step(recent):
        recent = recent.astype(jnp.float32)
        return jnp.concatenate([recent[step] for step in range(step_count)], axis=0)

    moved_query = by_head(moved_ref[0, :, :head_count, :])
    moved_key = by_step(moved_ref[0, :, head_count : head_count + kv_count, :])
    moved_value = by_step(moved_ref[0, :, head_count + kv_count :, :])
    recent_shape = (kv_count * token_rows, step_count * kv_count)
    token = lax.broadcasted_iota(jnp.int32, recent_shape, 0)
    columns = lax.broadcasted_iota(jnp.int32, recent_shape, 1)
    seen = (token // token_rows == columns % kv_count) & (
        columns // kv_count <= (token % token_rows) // group_size
    )

    own_rows = kv_count * token_rows
    together = math.gcd(row_count, 2)

    @pl.loop(0, row_count // together)
    def _(first):
        rows = [first * together + member for member in range(together)]
        members = range(together)
        lengths = [lengths_ref[own_index, row] for row in rows]
        queries, recent_values, recent = [], [], []
        for row in rows:
            moved = row == moved_row
            query = jnp.where(moved, moved_query, by_head(query_ref[row])).astype(jnp.bfloat16)
            recent_key = jnp.where(moved, moved_key, by_step(recent_key_ref[row]))
            recent_value = jnp.where(moved, moved_value, by_step(recent_value_ref[row]))
            queries.append(query)
            recent_values.append(recent_value.astype(jnp.bfloat16))
            products = lax.dot_general(
                query,
                recent_key.astype(jnp.bfloat16),
                contract_last,
                preferred_element_type=jnp.float32,
            )
            recent.append(jnp.where(seen, products * score_scale, masked_score))
        recent = jnp.concatenate(recent, axis=0)

        def attend(used):
            places = [[table_ref[block, row] for block in range(used)] for row in rows]
            shape = (own_rows, block_len)
            length = jnp.concatenate([jnp.full(shape, own, jnp.int32) for own in lengths], axis=0)
            position = lax.broadcasted_iota(jnp.int32, length.shape, 1)
            scores = []
            for block in range(used):
                products = [
                    lax.dot_general(
                        queries[member][head * token_rows : (head + 1) * token_rows],
                        key_ref[places[member][block], head],
                        contract_last,
                        preferred_element_type=jnp.float32,
                    )
                    for member in members
                    for head in heads
                ]
                products = jnp.concatenate(products, axis=0) * score_scale
                here = position + block * block_len < length
                scores.append(jnp.where(here, products, masked_score))
            highest = functools.reduce(jnp.maximum, scores)
            highest = jnp.maximum(
                jnp.max(highest, axis=1, keepdims=True), jnp.max(recent, axis=1, keepdims=True)
            )
            weights = [jnp.exp(score - highest) for score in scores]
            recent_weight = jnp.exp(recent - highest)
            denominator = jnp.sum(functools.reduce(jnp.add, weights), axis=1, keepdims=True)
            denominator += jnp.sum(recent_weight, axis=1, keepdims=True)
            scale = 1.0 / denominator
            weights = [(weight * scale).astype(jnp.bfloat16) for weight in weights]
            recent_weight = (recent_weight * scale).astype(jnp.bfloat16)
            for member in members:
                start = member * own_rows
                total = jnp.dot(
                    recent_weight[start : start + own_rows],
                    recent_values[member],
                    preferred_element_type=jnp.float32,
                )
                sums = []
                for head in heads:
                    own = slice(head * token_rows, (head + 1) * token_rows)
                    part = total[own]
                    for block in range(used):
                        part += jnp.dot(
                            weights[block][start + own.start : start + own.stop],
                            value_ref[places[member][block], head],
                            preferred_element_type=jnp.float32,
                        )
                    sums.append(part)
                total = jnp.concatenate(sums, axis=0)
                total = total.reshape(kv_count, step_count, group_size, head_width)
                total = total.transpose(1, 0, 2, 3).reshape(step_count, head_count, head_width)
                out_ref[rows[member]] = total.astype(out_ref.dtype)

        longest = functools.reduce(jnp.maximum, lengths)
        most = [1 << power for power in range(block_count.bit_length())]
        most = [used for used in most if used < block_count] + [block_count]
        for fewer, used in zip([0] + most, most):
            fits = (longest > fewer * block_len) & (longest <= used * block_len)
            pl.when(fits)(functools.partial(attend, used))


def attend_rows(
    key_pool, value_pool, block_table, lengths, pairs, queries, recent_keys, recent_values, moved_tokens
):
    block_count = block_table.shape[1]
    smem = pl.BlockSpec(memory_space=pltpu.SMEM)
    vmem = pl.BlockSpec(memory_space=pltpu.VMEM)
    return pl.pallas_call(
        attend_kernel,
        out_shape=jax.ShapeDtypeStruct(queries.shape, queries.dtype),
        in_specs=[smem, smem, smem, vmem, vmem, vmem, vmem, vmem, vmem],
        out_specs=vmem,
        compiler_params=pltpu.CompilerParams(vmem_limit_bytes=24 * 1024 * 1024),
        cost_estimate=pl.CostEstimate(flops=1, bytes_accessed=1, transcendentals=1),
        name="attend",
    )(
        lengths, block_table.T, pairs, key_pool, value_pool, queries, recent_keys, recent_values,
        moved_tokens,
    )


def guest_block(blocks, length, recent_rows):
    block_count, kv_count, block_len, head_width = blocks.shape
    position = (
        jnp.arange(block_count, dtype=jnp.int32)[:, None] * block_len
        + jnp.arange(block_len, dtype=jnp.int32)[None, :]
    )
    position = position[:, None, :, None]
    filled = jnp.where(position < length, blocks, jnp.zeros_like(blocks))
    for step_index in range(recent_rows.shape[0]):
        filled = jnp.where(
            position == length + step_index, recent_rows[step_index][None, :, None, :], filled
        )
    return filled


def pick_kernel(
    half_cycle, step_count, pairs_ref, table_ref, lengths_ref, key_ref, value_ref,
    facts_out, keys_out, values_out, sems,
):
    own_index = lax.axis_index("inst")
    row = lax.rem(own_index, half_cycle)
    request = pairs_ref[row, 1]
    blocks = table_ref.shape[0]
    copies = []
    for block in range(blocks):
        place = table_ref[block, request]
        copies.append(pltpu.make_async_copy(key_ref.at[place], keys_out.at[block], sems.at[block]))
        copies.append(
            pltpu.make_async_copy(value_ref.at[place], values_out.at[block], sems.at[blocks + block])
        )
    for copy in copies:
        copy.start()
    first = row - lax.rem(row, 2)
    second = jnp.minimum(first + 1, half_cycle - 1)
    facts_out[0] = (pairs_ref[first, 0] >= half_cycle).astype(jnp.int32) + 2 * (
        pairs_ref[second, 0] >= half_cycle
    ).astype(jnp.int32)
    moved_length = lengths_ref[pairs_ref[row, 0], request]
    facts_out[1] = jnp.where(pairs_ref[row, 2] == own_index, moved_length, -step_count)
    for copy in copies:
        copy.wait()


def pick_moved(key_pool, value_pool, block_table, lengths, pairs, half_cycle, step_count):
    blocks = block_table.shape[1]
    shape = jax.ShapeDtypeStruct((blocks,) + key_pool.shape[1:], key_pool.dtype)
    smem = pl.BlockSpec(memory_space=pltpu.SMEM)
    vmem = pl.BlockSpec(memory_space=pltpu.VMEM)
    pool = pl.BlockSpec(memory_space=pltpu.HBM)
    return pl.pallas_call(
        functools.partial(pick_kernel, half_cycle, step_count),
        out_shape=(jax.ShapeDtypeStruct((2,), jnp.int32), shape, shape),
        in_specs=[smem, smem, smem, pool, pool],
        out_specs=(smem, vmem, vmem),
        scratch_shapes=[pltpu.SemaphoreType.DMA((2 * blocks,))],
        name="pick_moved",
    )(pairs, block_table.T, lengths, key_pool, value_pool)


def plan_of(pattern, half_cycle):
    straight, to_neighbour, from_neighbour = [], [], []
    for low in range(half_cycle):
        ends = (low, low + half_cycle)
        source, target = ends[::-1] if pattern >> (low % 2) & 1 else ends
        straight.append((source, target))
        to_neighbour.append((source, source ^ 1))
        from_neighbour.append((source ^ 1, target))
    return straight, to_neighbour, from_neighbour


def shards(
    key_pool,
    value_pool,
    block_table,
    lengths,
    pairs,
    queries,
    new_keys,
    new_values,
    guest_queries,
    guest_new_keys,
    guest_new_values,
    *,
    relayed,
):
    half_cycle = lax.axis_size("inst") // 2
    step_count = queries.shape[1]
    guest_tokens = jnp.concatenate([guest_queries, guest_new_keys, guest_new_values], axis=2)
    moved_tokens = passed_along(guest_tokens, "inst", half_cycle)
    facts, send_keys, send_values = pick_moved(
        key_pool, value_pool, block_table, lengths, pairs, half_cycle, step_count
    )

    def finish(send, operands):
        (
            key_pool, value_pool, block_table, lengths, pairs, queries, new_keys, new_values,
            moved_tokens, guest_new_keys, guest_new_values, facts, send_keys, send_values,
        ) = operands
        got_keys, got_values = send(send_keys, send_values)
        attended = attend_rows(
            key_pool, value_pool, block_table, lengths, pairs, queries, new_keys, new_values, moved_tokens
        )
        guest_length = facts[1]
        guest_keys = guest_block(got_keys, guest_length, guest_new_keys[0])
        guest_keys, *got_values = lax.optimization_barrier((guest_keys, *got_values))
        got_values = got_values[0] if len(got_values) == 1 else jnp.concatenate(got_values, axis=0)
        guest_values = guest_block(got_values, guest_length, guest_new_values[0])
        return (attended, guest_keys, guest_values)

    def send_both_ways(*arrays):
        got_keys, got_values = (passed_along(array, "inst", half_cycle) for array in arrays)
        return got_keys, [got_values]

    def send_one_way(pattern, keys, values):
        straight, to_neighbour, from_neighbour = plan_of(pattern, half_cycle)
        got_keys = lax.ppermute(keys, "inst", straight)
        if pattern in (0, 3):
            return got_keys, [lax.ppermute(values, "inst", straight)]
        half = values.shape[0] // 2
        parts = []
        for part in (values[:half], values[half:]):
            relayed = lax.ppermute(part, "inst", to_neighbour)
            parts.append(lax.ppermute(relayed, "inst", from_neighbour))
        return got_keys, parts

    operands = (
        key_pool, value_pool, block_table, lengths, pairs, queries, new_keys, new_values,
        moved_tokens, guest_new_keys, guest_new_values, facts, send_keys, send_values,
    )
    if not relayed:
        return finish(send_both_ways, operands)
    branches = [
        functools.partial(finish, functools.partial(send_one_way, pattern)) for pattern in range(4)
    ]
    return lax.switch(facts[0], branches, operands)


def solution(mesh):
    relayed = mesh.shape["inst"] == 8
    return jax.shard_map(
        functools.partial(shards, relayed=relayed),
        mesh=mesh,
        in_specs=(
            P(("grp", "inst"), "tp", None, None),
            P(("grp", "inst"), "tp", None, None),
            P(("grp", "inst"), None),
            P("grp", None),
            P("grp", None),
            P(("grp", "inst"), None, "tp", None),
            P(("grp", "inst"), None, "tp", None),
            P(("grp", "inst"), None, "tp", None),
            P(("grp", "inst"), None, "tp", None),
            P(("grp", "inst"), None, "tp", None),
            P(("grp", "inst"), None, "tp", None),
        ),
        out_specs=(
            P(("grp", "inst"), None, "tp", None),
            P(("grp", "inst"), "tp", None, None),
            P(("grp", "inst"), "tp", None, None),
        ),
        check_vma=False,
    )
```
